32 devices in a mesh: row: 4 (over z), col: 8 (over y, x, core).
Axes of the slice: x: 2, y: 2, z: 4, core: 2. Of those that a mesh axis runs over, the one named last changes fastest.
Arguments:
- velocity: float32 [2, 512, 64, 384], P(None, 'col', 'row'), may hold values from -6 to 6
- synthesis: float32 [384, 384], replicated
- analysis: float32 [384, 384], replicated
- radial_eigen: float32 [384], replicated, may hold values from 0.05 to 4
- pair_list: int32 [64, 2], replicated, may hold values from 0 to 511, as said below
- owner_slot: int32 [64], replicated, may hold values from 0 to 63, each once
- freq_list: int32 [4], replicated, may hold values from 0 to 255
- snap_index: int32 [1], replicated, may hold values from 0 to 254
- block_dft: float32 [64, 4, 2, 384], P(('row', 'col')), may hold values from -6 to 6
- spectra: float32 [64, 4, 2, 384, 384], P(('row', 'col')), may hold values from -6 to 6
Outputs:
- velocity_next: float32 [2, 512, 64, 384], P(None, 'col', 'row')
- block_sums: float32 [64, 4, 2, 384], P(('row', 'col'))
- spectra_next: float32 [64, 4, 2, 384, 384], P(('row', 'col'))
The draws below stay inside these ranges and needn't reach their ends.
Inputs may be any that keep to these rules, and one draw needn't show every extreme that they name: `pair_list`: the pairs are distinct; the axial index is below 64 and the wavenumber below 512. Of the devices of the solver layout (row index times the size of col plus col index, holding axial indices row * 16 onward and wavenumbers col * 512 / size of col onward), each holds at most 8 selected pairs and some hold exactly 8. `owner_slot`: each slot once.
All inputs are finite; a program needn't handle non-finite values.
Results may differ from the reference program's by a relative error of at most 0.0001.
Values sent between devices are 32-bit elements; how exact they have to be, the bound alone decides.
A program may use at most 128 MiB of HBM per device.

```python
import math
import jax
import jax.numpy as jnp
from jax import lax

KX_DEV = 16
MTH = 512
NR = 384
SLOTS = 2
NFREQ = 4
NBLK = 256
NTH = 1536
NKX = 64
NSEL = 64
HOLD = 8
DEVICES = 32


def near_identity(key):
    spread = jax.random.normal(key, (NR, NR), jnp.float32) * (0.3 / NR ** 0.5)
    return jnp.eye(NR, dtype=jnp.float32) + spread


def draw_synthesis(key, part):
    return near_identity(jax.random.fold_in(key, 21))


def draw_analysis(key, part):
    return near_identity(jax.random.fold_in(key, 22))


def draw_pair_list(key, part):
    base = jax.random.fold_in(key, 31)
    order_key, cell_key, shuffle_key = jax.random.split(base, 3)
    col_count = DEVICES // (NKX // KX_DEV)
    modes_dev = MTH // col_count
    cells_each = KX_DEV * modes_dev
    device_order = jax.random.permutation(order_key, DEVICES)
    busy_count = DEVICES // 8
    first_block = busy_count * HOLD
    listing = jnp.arange(NSEL, dtype=jnp.int32)
    later = jnp.maximum(listing - first_block, 0)
    rank_of = jnp.where(listing < first_block, listing // HOLD, busy_count + later // (2 * SLOTS))
    within = jnp.where(listing < first_block, listing % HOLD, later % (2 * SLOTS))
    holder = device_order[rank_of]

    def first_cells(cell_one):
        return jax.random.permutation(cell_one, cells_each)[:HOLD]
    chosen = jax.vmap(first_cells)(jax.random.split(cell_key, DEVICES))
    cell = chosen[holder, within]
    axial = holder // col_count * KX_DEV + cell // modes_dev
    mode = holder % col_count * modes_dev + cell % modes_dev
    pairs = jnp.stack([axial, mode], axis=1).astype(jnp.int32)
    return pairs[jax.random.permutation(shuffle_key, NSEL)]


def touch_ends(array, stream_key, least, high):
    longest = array.shape.index(max(array.shape))
    spots = []
    for shift in (0, 1):
        where = [jax.random.randint(jax.random.fold_in(stream_key, axis), (), 0, length) for axis, length in enumerate(array.shape)]
        where[longest] = (where[longest] + shift) % array.shape[longest]
        spots.append(tuple(where))
    return array.at[spots[0]].set(least).at[spots[1]].set(high)


def level_of(key, dims, cuts, low, largest):
    def one(axis_at, parts):
        steps = jax.random.uniform(jax.random.fold_in(jax.random.fold_in(key, 6), axis_at), (parts,), jnp.float32, low / len(cuts), largest / len(cuts))
        return jnp.repeat(jnp.exp(steps), dims[axis_at] // parts).reshape((-1,) + (1,) * (len(dims) - axis_at - 1))

    factor_of = one(*cuts[0])
    for cut in cuts[1:]:
        factor_of = factor_of * one(*cut)
    return factor_of


def bell_draw(own_key, dims, width, reach, pieces=(), kind=jnp.bfloat16):
    entries = width * jax.random.normal(own_key, dims, jnp.float32)
    if pieces:
        entries = entries * level_of(own_key, dims, pieces, -0.22, 0.18)
    return jnp.clip(entries, -reach, reach).astype(kind)


def setup_inputs(seed: int = 0) -> dict:
    streams_of = jax.random.split(jax.random.key(seed), 11)
    velocity = bell_draw(streams_of[0], (2, MTH, NKX, NR), 1.0, 6.0, ((1, 8), (2, 4)), jnp.float32)
    synthesis = draw_synthesis(jax.random.fold_in(streams_of[10], 71), 0)
    analysis = draw_analysis(jax.random.fold_in(streams_of[10], 71), 0)
    radial_eigen = jnp.clip(jnp.exp(jax.random.uniform(streams_of[3], (NR,), jnp.float32, math.log(0.05), math.log(4.0))), 0.05, 4.0)
    pair_list = draw_pair_list(jax.random.fold_in(streams_of[10], 71), 0)
    owner_slot = jax.random.permutation(streams_of[5], NSEL).astype(jnp.int32)
    freq_list = touch_ends(jax.random.randint(streams_of[6], (NFREQ,), 0, NBLK), jax.random.fold_in(streams_of[6], 1), 0, NBLK - 1).astype(jnp.int32)
    snap_index = jax.random.randint(streams_of[7], (1,), 0, NBLK - 1).astype(jnp.int32)
    block_dft = bell_draw(streams_of[8], (NSEL, NFREQ, 2, NR), 1.0, 6.0, ((0, 32),), jnp.float32)
    spectra = bell_draw(streams_of[9], (NSEL, NFREQ, 2, NR, NR), 1.0, 6.0, ((0, 32),), jnp.float32)
    return dict(velocity=velocity, synthesis=synthesis, analysis=analysis, radial_eigen=radial_eigen, pair_list=pair_list, owner_slot=owner_slot, freq_list=freq_list, snap_index=snap_index, block_dft=block_dft, spectra=spectra)


viscosity = 4e-06
axial_scale = 2.0
nonlinear_gain = 0.1
highest = lax.Precision.HIGHEST

def circle_forcing(current):
    spectrum = current[0] + 1j * current[1]
    physical = jnp.fft.irfft(spectrum, n=NTH, axis=0) * (NTH / math.sqrt(MTH))
    squared = physical * physical
    folded = jnp.fft.rfft(squared, axis=0)[:MTH] * (math.sqrt(MTH) / NTH)
    keep_mask = (jnp.arange(MTH) > 0)[:, None, None]
    real_part = jnp.where(keep_mask, folded.real, 0.0)
    imag_part = jnp.where(keep_mask, folded.imag, 0.0)
    return jnp.stack([real_part, imag_part]).astype(jnp.float32)

def radial_solve(rhs, analysis, synthesis, damping):
    coeffs = jnp.einsum('cmkr,rq->cmkq', rhs, analysis, precision=highest) * damping[None]
    return jnp.einsum('cmkq,qs->cmks', coeffs, synthesis, precision=highest)

def window_terms(freq_list, snap_now):
    position = snap_now.astype(jnp.float32)
    window = 0.54 - 0.46 * jnp.cos(2.0 * math.pi * position / NBLK)
    phase = (freq_list * snap_now % NBLK).astype(jnp.float32) * (2.0 * math.pi / NBLK)
    return (window * jnp.cos(phase), -window * jnp.sin(phase))

def add_snapshot(block, snapshot, real_w, imag_w):
    real_new = block[:, :, 0] + real_w[None, :, None] * snapshot[0][:, None, :] - imag_w[None, :, None] * snapshot[1][:, None, :]
    imag_new = block[:, :, 1] + real_w[None, :, None] * snapshot[1][:, None, :] + imag_w[None, :, None] * snapshot[0][:, None, :]
    return jnp.stack([real_new, imag_new], axis=2)

def spectral_update(spectrum_one, old_block, new_block):
    old_real, old_imag = (old_block[:, 0], old_block[:, 1])
    new_real, new_imag = (new_block[:, 0], new_block[:, 1])
    left_real = jnp.stack([new_real, new_imag, old_real, old_imag], axis=1)
    left_imag = jnp.stack([new_imag, -new_real, old_imag, -old_real], axis=1)
    left = jnp.stack([left_real, left_imag], axis=1)
    right = jnp.stack([new_real, new_imag, -old_real, -old_imag], axis=1)
    return spectrum_one + jnp.einsum('fckr,fkq->fcrq', left, right, precision=highest)

def slot_update(items):
    return spectral_update(items[0], items[1], items[2])

def reference(velocity, synthesis, analysis, radial_eigen, pair_list, owner_slot, freq_list, snap_index, block_dft, spectra):
    axial_ids = jnp.arange(NKX).astype(jnp.float32) * axial_scale
    mode_ids = jnp.arange(MTH).astype(jnp.float32)
    damping = 1.0 / (1.0 + viscosity * (axial_ids[None, :, None] ** 2 + mode_ids[:, None, None] ** 2) + radial_eigen[None, None, :])
    current = velocity
    snapshots = []
    for section_index in range(2):
        rhs = current - nonlinear_gain * circle_forcing(current)
        current = radial_solve(rhs, analysis, synthesis, damping)
        snapshots.append(current)
    slot_ids = jnp.arange(NSEL, dtype=jnp.int32)
    pair_of_slot = jnp.zeros((NSEL,), jnp.int32).at[owner_slot].set(slot_ids)
    axial_sel = pair_list[pair_of_slot, 0].astype(jnp.int32)
    mode_sel = pair_list[pair_of_slot, 1].astype(jnp.int32)
    block = block_dft
    for section_index in range(2):
        picked = snapshots[section_index][:, mode_sel, axial_sel, :]
        real_w, imag_w = window_terms(freq_list, snap_index[0] + section_index)
        block = add_snapshot(block, picked, real_w, imag_w)
    spectra_next = lax.map(slot_update, (spectra, block_dft, block))
    return (current, block, spectra_next)
```

```python
import math

import numpy as np

import jax
import jax.numpy as jnp
from jax import lax
from jax.sharding import PartitionSpec as P

NBLK = 256


viscosity = 4e-06
axial_scale = 2.0
nonlinear_gain = 0.1
highest = lax.Precision.HIGHEST
high = lax.Precision.HIGH


def quarter_tables(mode_count):
    points = 3 * mode_count
    quarter = points // 4
    mode_ids = np.arange(mode_count).reshape(-1, 2).T
    point_ids = 2 * np.arange(quarter) + 1
    angle = (point_ids[None, :, None] * mode_ids[:, None, :] % (2 * points)) * (math.pi / points)
    weight = np.where(mode_ids == 0, 1.0, 2.0)[:, None, :] * mode_count**-0.5
    keeping = np.where(mode_ids == 0, 0.0, 4.0 * math.sqrt(mode_count) / points)[:, None, :]
    both = np.stack([np.cos(angle), -np.sin(angle)])
    return (both * weight).astype(np.float32), (both * keeping).astype(np.float32)


def circle_forcing(split, synth_table, anal_table):
    part = jnp.einsum("cpjm,cmpkr->cpjkr", synth_table, split, precision=high)
    ce, co, se, so = part[0, 0], part[0, 1], part[1, 0], part[1, 1]
    pairs = jnp.stack(
        [
            jnp.stack([ce * ce + co * co + se * se + so * so, 2.0 * (ce * co + se * so)]),
            jnp.stack([2.0 * (ce * se + co * so), 2.0 * (ce * so + co * se)]),
        ]
    )
    return jnp.einsum("cpjm,cpjkr->cmpkr", anal_table, pairs, precision=high)


def damping_for(axial_int, mode_int, radial_eigen):
    axial_ids = axial_int.astype(jnp.float32) * axial_scale
    mode_ids = mode_int.astype(jnp.float32)
    return 1.0 / (
        1.0
        + viscosity * (axial_ids[None, :, None] ** 2 + mode_ids[:, None, None] ** 2)
        + radial_eigen[None, None, :]
    )


def radial_apply(rhs, analysis, synthesis, damping):
    radial_pts = rhs.shape[-1]
    coeffs = (
        jnp.dot(rhs.reshape(-1, radial_pts), analysis, precision=high).reshape(rhs.shape)
        * damping[None]
    )
    return jnp.dot(coeffs.reshape(-1, radial_pts), synthesis, precision=high).reshape(rhs.shape)


def window_terms(freq_list, snap_now):
    position = snap_now.astype(jnp.float32)
    window = 0.54 - 0.46 * jnp.cos(2.0 * math.pi * position / NBLK)
    phase = (freq_list * snap_now % NBLK).astype(jnp.float32) * (2.0 * math.pi / NBLK)
    return (window * jnp.cos(phase), -window * jnp.sin(phase))


def add_snapshot(block, snapshot, real_w, imag_w):
    real_new = (
        block[:, :, 0]
        + real_w[None, :, None] * snapshot[0][:, None, :]
        - imag_w[None, :, None] * snapshot[1][:, None, :]
    )
    imag_new = (
        block[:, :, 1]
        + real_w[None, :, None] * snapshot[1][:, None, :]
        + imag_w[None, :, None] * snapshot[0][:, None, :]
    )
    return jnp.stack([real_new, imag_new], axis=2)


def spectral_update(spectrum_one, old_block, new_block):
    old_real, old_imag = (old_block[:, 0], old_block[:, 1])
    new_real, new_imag = (new_block[:, 0], new_block[:, 1])
    left_real = jnp.stack([new_real, new_imag, old_real, old_imag], axis=1)
    left_imag = jnp.stack([new_imag, -new_real, old_imag, -old_real], axis=1)
    left = jnp.stack([left_real, left_imag], axis=1)
    right = jnp.stack([new_real, new_imag, -old_real, -old_imag], axis=1)
    return spectrum_one + jnp.einsum("fckr,fkq->fcrq", left, right, precision=highest)


def local(
    velocity,
    synthesis,
    analysis,
    radial_eigen,
    pair_list,
    owner_slot,
    freq_list,
    snap_index,
    block_dft,
    spectra,
):
    modes_dev = velocity.shape[1]
    axial_dev = velocity.shape[2]
    col_count = lax.axis_size("col")
    modes_all = modes_dev * col_count
    synth_table, anal_table = quarter_tables(modes_all)
    row_index = lax.axis_index("row")
    col_index = lax.axis_index("col")
    row_count = lax.axis_size("row")
    share = axial_dev // col_count
    base = row_index * axial_dev + col_index * share
    selected = pair_list.shape[0]
    slot_ids = jnp.arange(selected, dtype=jnp.int32)
    of_slot = (owner_slot[None, :] == slot_ids[:, None]).astype(jnp.int32)
    chosen = jnp.sum(of_slot[:, :, None] * pair_list[None], axis=1)
    axial_sel, mode_sel = (chosen[:, 0] - base, chosen[:, 1])
    hit_axial = axial_sel[:, None] == jnp.arange(share, dtype=jnp.int32)[None, :]
    hit_mode = mode_sel[:, None] == jnp.arange(modes_all, dtype=jnp.int32)[None, :]
    pick = (hit_mode[:, :, None] & hit_axial[:, None, :]).astype(jnp.float32)
    state = lax.all_to_all(velocity, "col", split_axis=2, concat_axis=1, tiled=True)
    local_axial = base + jnp.arange(share, dtype=jnp.int32)
    local_damping = damping_for(local_axial, jnp.arange(modes_all, dtype=jnp.int32), radial_eigen)
    picked = []
    for section_index in range(2):
        split = state.reshape(2, modes_all // 2, 2, share, -1)
        rhs = state - nonlinear_gain * circle_forcing(split, synth_table, anal_table).reshape(state.shape)
        state = radial_apply(rhs, analysis, synthesis, local_damping)
        picked.append(jnp.einsum("smk,cmkr->csr", pick, state, precision=highest))
    dense = jnp.stack(picked).reshape(2, 2, row_count, col_count, -1, state.shape[-1])
    part = jnp.sum(lax.all_to_all(dense, "col", split_axis=3, concat_axis=3, tiled=True), axis=3)
    mine = jnp.sum(lax.all_to_all(part, "row", split_axis=2, concat_axis=2, tiled=True), axis=2)
    current = lax.all_to_all(state, "col", split_axis=1, concat_axis=2, tiled=True)
    block = block_dft
    for section_index in range(2):
        real_w, imag_w = window_terms(freq_list, snap_index[0] + section_index)
        block = add_snapshot(block, mine[section_index], real_w, imag_w)
    spectra_next = jax.vmap(spectral_update)(spectra, block_dft, block)
    return (current, block, spectra_next)


def solution(mesh):
    return jax.shard_map(
        local,
        mesh=mesh,
        in_specs=(
            P(None, "col", "row", None),
            P(),
            P(),
            P(),
            P(),
            P(),
            P(),
            P(),
            P(("row", "col"), None, None, None),
            P(("row", "col"), None, None, None, None),
        ),
        out_specs=(
            P(None, "col", "row", None),
            P(("row", "col"), None, None, None),
            P(("row", "col"), None, None, None, None),
        ),
        check_vma=False,
    )
```

```python
import math

import numpy as np

import jax
import jax.numpy as jnp
import ml_dtypes
from jax import lax
from jax.experimental import pallas as pl
from jax.experimental.pallas import tpu as pltpu
from jax.sharding import PartitionSpec as P

NBLK = 256


viscosity = 4e-06
axial_scale = 2.0
nonlinear_gain = 0.1
highest = lax.Precision.HIGHEST


def quarter_tables(mode_count):
    points = 3 * mode_count
    quarter = points // 4
    mode_ids = np.arange(mode_count).reshape(-1, 2).T
    point_ids = 2 * np.arange(quarter) + 1
    angle = (point_ids[None, :, None] * mode_ids[:, None, :] % (2 * points)) * (math.pi / points)
    weight = np.where(mode_ids == 0, 1.0, 2.0)[:, None, :] * mode_count**-0.5
    keeping = np.where(mode_ids == 0, 0.0, 4.0 * math.sqrt(mode_count) / points)[:, None, :]
    both = np.stack([np.cos(angle), -np.sin(angle)])
    return both * weight, np.swapaxes(both * keeping, 2, 3)


def halves(table):
    upper = table.astype(ml_dtypes.bfloat16)
    lower = (table - upper.astype(np.float64)).astype(ml_dtypes.bfloat16)
    return np.stack([upper, lower])


def split_two(value):
    upper = value.astype(jnp.bfloat16)
    return upper, (value - upper.astype(jnp.float32)).astype(jnp.bfloat16)


def dot(left, right):
    return jnp.dot(left, right, preferred_element_type=jnp.float32)


def dot_three(left, right):
    return dot(left[0], right[0]) + (dot(left[0], right[1]) + dot(left[1], right[0]))


def steps_kernel(
    field_ref, synth_ref, anal_ref, analysis_ref, synthesis_ref, damping_ref, pick_ref, out_ref, snaps_ref
):
    owners, _, _, _, each, radial_pts = field_ref.shape
    half = owners * each

    @pl.when(pl.program_id(0) == 0)
    def _():
        snaps_ref[...] = jnp.zeros_like(snaps_ref)

    out_ref[...] = field_ref[...]

    def step(section_index, carry):
        parts = []
        for c in range(2):
            for p in range(2):
                now = split_two(out_ref[:, 0, c, p].reshape(half, radial_pts))
                parts.append(dot_three((synth_ref[0, c, p], synth_ref[1, c, p]), now))
        ce, co, se, so = parts
        pairs = (
            (ce * ce + co * co + se * se + so * so, 2.0 * (ce * co + se * so)),
            (2.0 * (ce * se + co * so), 2.0 * (ce * so + co * se)),
        )
        to_eigen = split_two(analysis_ref[...])
        to_points = split_two(synthesis_ref[...])
        for c in range(2):
            snap = jnp.zeros(snaps_ref.shape[2:], jnp.float32)
            for p in range(2):
                forcing = dot_three((anal_ref[0, c, p], anal_ref[1, c, p]), split_two(pairs[c][p]))
                rhs = out_ref[:, 0, c, p].reshape(half, radial_pts) - nonlinear_gain * forcing
                coeffs = dot_three(split_two(rhs), to_eigen) * damping_ref[0, p]
                after = dot_three(split_two(coeffs), to_points)
                out_ref[:, 0, c, p] = after.reshape(owners, each, radial_pts)
                upper, lower = split_two(after)
                snap += dot(pick_ref[0, p], upper) + dot(pick_ref[0, p], lower)
            snaps_ref[section_index, c] += snap
        return carry

    lax.fori_loop(0, 2, step, 0)


def run_steps(field, synth, anal, analysis, synthesis, damping, pick):
    owners, share, _, _, each, radial_pts = field.shape
    selected = pick.shape[2]

    def whole(array):
        return pl.BlockSpec(array.shape, lambda k: (0,) * array.ndim)

    def one(array):
        return pl.BlockSpec((1, *array.shape[1:]), lambda k: (k,) + (0,) * (array.ndim - 1))

    field_spec = pl.BlockSpec((owners, 1, 2, 2, each, radial_pts), lambda k: (0, k, 0, 0, 0, 0))
    return pl.pallas_call(
        steps_kernel,
        grid=(share,),
        in_specs=[
            field_spec, whole(synth), whole(anal), whole(analysis), whole(synthesis), one(damping), one(pick)
        ],
        out_specs=[field_spec, pl.BlockSpec((2, 2, selected, radial_pts), lambda k: (0, 0, 0, 0))],
        out_shape=[
            jax.ShapeDtypeStruct(field.shape, jnp.float32),
            jax.ShapeDtypeStruct((2, 2, selected, radial_pts), jnp.float32),
        ],
        compiler_params=pltpu.CompilerParams(vmem_limit_bytes=50 * 2**20),
    )(field, synth, anal, analysis, synthesis, damping, pick)


def window_terms(freq_list, snap_now):
    position = snap_now.astype(jnp.float32)
    window = 0.54 - 0.46 * jnp.cos(2.0 * math.pi * position / NBLK)
    phase = (freq_list * snap_now % NBLK).astype(jnp.float32) * (2.0 * math.pi / NBLK)
    return (window * jnp.cos(phase), -window * jnp.sin(phase))


def add_snapshot(block, snapshot, real_w, imag_w):
    real_new = (
        block[:, :, 0]
        + real_w[None, :, None] * snapshot[0][:, None, :]
        - imag_w[None, :, None] * snapshot[1][:, None, :]
    )
    imag_new = (
        block[:, :, 1]
        + real_w[None, :, None] * snapshot[1][:, None, :]
        + imag_w[None, :, None] * snapshot[0][:, None, :]
    )
    return jnp.stack([real_new, imag_new], axis=2)


def spectral_update(spectrum_one, old_block, new_block):
    old_real, old_imag = (old_block[:, 0], old_block[:, 1])
    new_real, new_imag = (new_block[:, 0], new_block[:, 1])
    left_real = jnp.stack([new_real, new_imag, old_real, old_imag], axis=1)
    left_imag = jnp.stack([new_imag, -new_real, old_imag, -old_real], axis=1)
    left = jnp.stack([left_real, left_imag], axis=1)
    right = jnp.stack([new_real, new_imag, -old_real, -old_imag], axis=1)
    return spectrum_one + jnp.einsum("fckr,fkq->fcrq", left, right, precision=highest)


def local(
    velocity,
    synthesis,
    analysis,
    radial_eigen,
    pair_list,
    owner_slot,
    freq_list,
    snap_index,
    block_dft,
    spectra,
):
    modes_dev = velocity.shape[1]
    axial_dev = velocity.shape[2]
    col_count = lax.axis_size("col")
    modes_all = modes_dev * col_count
    synth, anal = quarter_tables(modes_all)
    synth, anal = jnp.asarray(halves(synth)), jnp.asarray(halves(anal))
    row_index = lax.axis_index("row")
    col_index = lax.axis_index("col")
    row_count = lax.axis_size("row")
    share = axial_dev // col_count
    base = row_index * axial_dev + col_index * share
    selected = pair_list.shape[0]
    slot_ids = jnp.arange(selected, dtype=jnp.int32)
    of_slot = (owner_slot[None, :] == slot_ids[:, None]).astype(jnp.int32)
    chosen = jnp.sum(of_slot[:, :, None] * pair_list[None], axis=1)
    axial_sel, mode_sel = (chosen[:, 0] - base, chosen[:, 1])
    mode_ids = jnp.asarray(np.arange(modes_all, dtype=np.int32).reshape(-1, 2).T)
    hit_axial = axial_sel[None, :] == jnp.arange(share, dtype=jnp.int32)[:, None]
    hit_mode = mode_sel[None, :, None] == mode_ids[:, None, :]
    pick = (hit_axial[:, None, :, None] & hit_mode[None]).astype(jnp.bfloat16)
    axial_ids = (base + jnp.arange(share, dtype=jnp.int32)).astype(jnp.float32) * axial_scale
    damping = 1.0 / (
        1.0
        + viscosity
        * (axial_ids[:, None, None, None] ** 2 + mode_ids.astype(jnp.float32)[None, :, :, None] ** 2)
        + radial_eigen
    )
    radial_pts = velocity.shape[3]
    each = modes_dev // 2
    outgoing = velocity.reshape(2, each, 2, axial_dev, radial_pts).transpose(3, 0, 2, 1, 4)
    field = lax.all_to_all(
        outgoing.reshape(col_count, share, 2, 2, each, radial_pts), "col", split_axis=0, concat_axis=0, tiled=True
    )
    state, snaps = run_steps(field, synth, anal, analysis, synthesis, damping, pick)
    dense = snaps.reshape(2, 2, row_count, col_count, -1, radial_pts)
    part = jnp.sum(lax.all_to_all(dense, "col", split_axis=3, concat_axis=3, tiled=True), axis=3)
    mine = jnp.sum(lax.all_to_all(part, "row", split_axis=2, concat_axis=2, tiled=True), axis=2)
    back = lax.all_to_all(state, "col", split_axis=0, concat_axis=0, tiled=True)
    back = back.reshape(axial_dev, 2, 2, each, radial_pts).transpose(1, 3, 2, 0, 4)
    current = back.reshape(velocity.shape)
    block = block_dft
    for section_index in range(2):
        real_w, imag_w = window_terms(freq_list, snap_index[0] + section_index)
        block = add_snapshot(block, mine[section_index], real_w, imag_w)
    spectra_next = jax.vmap(spectral_update)(spectra, block_dft, block)
    return (current, block, spectra_next)


def solution(mesh):
    return jax.shard_map(
        local,
        mesh=mesh,
        in_specs=(
            P(None, "col", "row", None),
            P(),
            P(),
            P(),
            P(),
            P(),
            P(),
            P(),
            P(("row", "col"), None, None, None),
            P(("row", "col"), None, None, None, None),
        ),
        out_specs=(
            P(None, "col", "row", None),
            P(("row", "col"), None, None, None),
            P(("row", "col"), None, None, None, None),
        ),
        check_vma=False,
    )
```

```python
import math

import numpy as np

import jax
import jax.numpy as jnp
import ml_dtypes
from jax import lax
from jax.experimental import pallas as pl
from jax.experimental.pallas import tpu as pltpu
from jax.sharding import PartitionSpec as P

NBLK = 256


viscosity = 4e-06
axial_scale = 2.0
nonlinear_gain = 0.1
highest = lax.Precision.HIGHEST


def quarter_tables(mode_count):
    points = 3 * mode_count
    quarter = points // 4
    mode_ids = np.arange(mode_count).reshape(-1, 2).T
    point_ids = 2 * np.arange(quarter) + 1
    angle = (point_ids[None, :, None] * mode_ids[:, None, :] % (2 * points)) * (math.pi / points)
    weight = np.where(mode_ids == 0, 1.0, 2.0)[:, None, :] * mode_count**-0.5
    keeping = np.where(mode_ids == 0, 0.0, 4.0 * math.sqrt(mode_count) / points)[:, None, :]
    both = np.stack([np.cos(angle), -np.sin(angle)])
    return both * weight, np.swapaxes(both * keeping, 2, 3)


def halves(table):
    upper = table.astype(ml_dtypes.bfloat16)
    lower = (table - upper.astype(np.float64)).astype(ml_dtypes.bfloat16)
    return np.stack([upper, lower])


def split_two(value):
    upper = value.astype(jnp.bfloat16)
    return upper, (value - upper.astype(jnp.float32)).astype(jnp.bfloat16)


def dot(left, right):
    return jnp.dot(left, right, preferred_element_type=jnp.float32)


def dot_three(left, right):
    return dot(left[0], right[0]) + (dot(left[0], right[1]) + dot(left[1], right[0]))


def steps_kernel(
    field_ref, synth_ref, anal_ref, analysis_ref, synthesis_ref, damping_ref, pick_ref, out_ref, snaps_ref
):
    owners, _, _, _, each, radial_pts = field_ref.shape
    half = owners * each

    @pl.when(pl.program_id(0) == 0)
    def _():
        snaps_ref[...] = jnp.zeros_like(snaps_ref)

    out_ref[...] = field_ref[...]

    def step(section_index, carry):
        parts = []
        for c in range(2):
            for p in range(2):
                now = split_two(out_ref[:, 0, c, p].reshape(half, radial_pts))
                parts.append(dot_three((synth_ref[0, c, p], synth_ref[1, c, p]), now))
        ce, co, se, so = parts
        pairs = (
            (ce * ce + co * co + se * se + so * so, 2.0 * (ce * co + se * so)),
            (2.0 * (ce * se + co * so), 2.0 * (ce * so + co * se)),
        )
        to_eigen = split_two(analysis_ref[...])
        to_points = split_two(synthesis_ref[...])
        for c in range(2):
            snap = jnp.zeros(snaps_ref.shape[2:], jnp.float32)
            for p in range(2):
                forcing = dot_three((anal_ref[0, c, p], anal_ref[1, c, p]), split_two(pairs[c][p]))
                rhs = out_ref[:, 0, c, p].reshape(half, radial_pts) - nonlinear_gain * forcing
                coeffs = dot_three(split_two(rhs), to_eigen) * damping_ref[0, p]
                after = dot_three(split_two(coeffs), to_points)
                out_ref[:, 0, c, p] = after.reshape(owners, each, radial_pts)
                upper, lower = split_two(after)
                snap += dot(pick_ref[0, p], upper) + dot(pick_ref[0, p], lower)
            snaps_ref[section_index, c] += snap
        return carry

    lax.fori_loop(0, 2, step, 0)


def run_steps(field, synth, anal, analysis, synthesis, damping, pick):
    owners, share, _, _, each, radial_pts = field.shape
    selected = pick.shape[2]

    def whole(array):
        return pl.BlockSpec(array.shape, lambda k: (0,) * array.ndim)

    def one(array):
        return pl.BlockSpec((1, *array.shape[1:]), lambda k: (k,) + (0,) * (array.ndim - 1))

    field_spec = pl.BlockSpec((owners, 1, 2, 2, each, radial_pts), lambda k: (0, k, 0, 0, 0, 0))
    return pl.pallas_call(
        steps_kernel,
        grid=(share,),
        in_specs=[
            field_spec, whole(synth), whole(anal), whole(analysis), whole(synthesis), one(damping), one(pick)
        ],
        out_specs=[field_spec, pl.BlockSpec((2, 2, selected, radial_pts), lambda k: (0, 0, 0, 0))],
        out_shape=[
            jax.ShapeDtypeStruct(field.shape, jnp.float32),
            jax.ShapeDtypeStruct((2, 2, selected, radial_pts), jnp.float32),
        ],
        cost_estimate=pl.CostEstimate(
            flops=share * 14 * 10**9, bytes_accessed=share * 8 * 10**6, transcendentals=0
        ),
        compiler_params=pltpu.CompilerParams(vmem_limit_bytes=50 * 2**20),
    )(field, synth, anal, analysis, synthesis, damping, pick)


def window_terms(freq_list, snap_now):
    position = snap_now.astype(jnp.float32)
    window = 0.54 - 0.46 * jnp.cos(2.0 * math.pi * position / NBLK)
    phase = (freq_list * snap_now % NBLK).astype(jnp.float32) * (2.0 * math.pi / NBLK)
    return (window * jnp.cos(phase), -window * jnp.sin(phase))


def add_snapshot(block, snapshot, real_w, imag_w):
    real_new = (
        block[:, :, 0]
        + real_w[None, :, None] * snapshot[0][:, None, :]
        - imag_w[None, :, None] * snapshot[1][:, None, :]
    )
    imag_new = (
        block[:, :, 1]
        + real_w[None, :, None] * snapshot[1][:, None, :]
        + imag_w[None, :, None] * snapshot[0][:, None, :]
    )
    return jnp.stack([real_new, imag_new], axis=2)


def spectral_update(spectrum_one, old_block, new_block):
    old_real, old_imag = (old_block[:, 0], old_block[:, 1])
    new_real, new_imag = (new_block[:, 0], new_block[:, 1])
    left_real = jnp.stack([new_real, new_imag, old_real, old_imag], axis=1)
    left_imag = jnp.stack([new_imag, -new_real, old_imag, -old_real], axis=1)
    left = jnp.stack([left_real, left_imag], axis=1)
    right = jnp.stack([new_real, new_imag, -old_real, -old_imag], axis=1)
    return spectrum_one + jnp.einsum("fckr,fkq->fcrq", left, right, precision=highest)


def local(
    velocity,
    synthesis,
    analysis,
    radial_eigen,
    pair_list,
    owner_slot,
    freq_list,
    snap_index,
    block_dft,
    spectra,
):
    modes_dev = velocity.shape[1]
    axial_dev = velocity.shape[2]
    col_count = lax.axis_size("col")
    modes_all = modes_dev * col_count
    synth, anal = quarter_tables(modes_all)
    synth, anal = jnp.asarray(halves(synth)), jnp.asarray(halves(anal))
    row_index = lax.axis_index("row")
    col_index = lax.axis_index("col")
    row_count = lax.axis_size("row")
    share = axial_dev // col_count
    base = row_index * axial_dev + col_index * share
    selected = pair_list.shape[0]
    slot_ids = jnp.arange(selected, dtype=jnp.int32)
    of_slot = (owner_slot[None, :] == slot_ids[:, None]).astype(jnp.int32)
    chosen = jnp.sum(of_slot[:, :, None] * pair_list[None], axis=1)
    axial_sel, mode_sel = (chosen[:, 0] - base, chosen[:, 1])
    mode_ids = jnp.asarray(np.arange(modes_all, dtype=np.int32).reshape(-1, 2).T)
    hit_axial = axial_sel[None, :] == jnp.arange(share, dtype=jnp.int32)[:, None]
    hit_mode = mode_sel[None, :, None] == mode_ids[:, None, :]
    pick = (hit_axial[:, None, :, None] & hit_mode[None]).astype(jnp.bfloat16)
    axial_ids = (base + jnp.arange(share, dtype=jnp.int32)).astype(jnp.float32) * axial_scale
    damping = 1.0 / (
        1.0
        + viscosity
        * (axial_ids[:, None, None, None] ** 2 + mode_ids.astype(jnp.float32)[None, :, :, None] ** 2)
        + radial_eigen
    )
    radial_pts = velocity.shape[3]
    each = modes_dev // 2
    outgoing = velocity.reshape(2, each, 2, axial_dev, radial_pts).transpose(3, 0, 2, 1, 4)
    outgoing = outgoing.reshape(col_count, share, 2, 2, each, radial_pts)
    fields = [
        lax.all_to_all(outgoing[:, k : k + 1], "col", split_axis=0, concat_axis=0, tiled=True)
        for k in range(share)
    ]
    done = [
        run_steps(fields[k], synth, anal, analysis, synthesis, damping[k : k + 1], pick[k : k + 1])
        for k in range(share)
    ]
    snaps = sum(snap for _, snap in done)
    dense = snaps.reshape(2, 2, row_count, col_count, -1, radial_pts)
    part = jnp.sum(lax.all_to_all(dense, "col", split_axis=3, concat_axis=3, tiled=True), axis=3)
    mine = jnp.sum(lax.all_to_all(part, "row", split_axis=2, concat_axis=2, tiled=True), axis=2)
    back = jnp.concatenate(
        [lax.all_to_all(state, "col", split_axis=0, concat_axis=0, tiled=True) for state, _ in done], axis=1
    )
    back = back.reshape(axial_dev, 2, 2, each, radial_pts).transpose(1, 3, 2, 0, 4)
    current = back.reshape(velocity.shape)
    block = block_dft
    for section_index in range(2):
        real_w, imag_w = window_terms(freq_list, snap_index[0] + section_index)
        block = add_snapshot(block, mine[section_index], real_w, imag_w)
    spectra_next = jax.vmap(spectral_update)(spectra, block_dft, block)
    return (current, block, spectra_next)


def solution(mesh):
    return jax.shard_map(
        local,
        mesh=mesh,
        in_specs=(
            P(None, "col", "row", None),
            P(),
            P(),
            P(),
            P(),
            P(),
            P(),
            P(),
            P(("row", "col"), None, None, None),
            P(("row", "col"), None, None, None, None),
        ),
        out_specs=(
            P(None, "col", "row", None),
            P(("row", "col"), None, None, None),
            P(("row", "col"), None, None, None, None),
        ),
        check_vma=False,
    )
```
